32 devices in a mesh: tm: 8 (over z, x), gauge: 4 (over y, core).
Axes of the slice: x: 2, y: 2, z: 4, core: 2. Of those that a mesh axis runs over, the one named last changes fastest.
Arguments:
- records: bfloat16 [65536, 1536], P('tm', 'gauge'), may hold values from -400 to 400
- offsets: int32 [64], P('tm'), may hold values from 0 to 960
- column_map: int32 [1536], replicated, may hold values from 0 to 1535, each once
- angles: float32 [512], replicated, may hold values from -3.140625 to 3.140625
Outputs:
- factor: float32 [1536, 1536], replicated
The draws below stay inside these ranges and needn't reach their ends.
All inputs are finite; a program needn't handle non-finite values.
Results may differ from the reference program's by a relative error of at most 0.0014.
Values may be sent and summed in bfloat16 or wider, within the bound.
A program may use at most 128 MiB of HBM per device.

```python
import math
import jax
import jax.numpy as jnp
from jax import lax

GAUGES = 512
COLS = 1536
BLOCK = 1024
BAND = 64
SAMPLES = 65536
NBLOCKS = 64


def draw_records(key, part):
    keys = jax.random.split(key, 4)
    nblocks = SAMPLES // BLOCK
    scales = jnp.exp(jax.random.uniform(keys[0], (COLS,), jnp.float32, 0.0, math.log(10.0)))
    noise = jnp.clip(jax.random.normal(keys[1], (SAMPLES, COLS), jnp.float32), -5.0, 5.0)
    level = 3.0 * jnp.clip(jax.random.normal(keys[2], (nblocks, 1, COLS), jnp.float32), -4.0, 4.0)
    slope = 4.0 * jnp.clip(jax.random.normal(keys[3], (nblocks, 1, COLS), jnp.float32), -4.0, 4.0)
    ramp = (jnp.arange(BLOCK, dtype=jnp.float32) / BLOCK - 0.5)[None, :, None]
    drift = (level + slope * ramp).reshape(SAMPLES, COLS)
    return (scales[None, :] * (noise + drift)).astype(jnp.bfloat16)


def touch_ends(values, own_key, smallest, largest):
    shape = values.shape
    index_at = [jax.random.randint(jax.random.fold_in(own_key, axis), (), 0, shape[axis]) for axis in range(len(shape))]
    values = values.at[tuple(index_at)].set(smallest)
    longest = shape.index(max(shape))
    index_at[longest] = (index_at[longest] + 1) % shape[longest]
    return values.at[tuple(index_at)].set(largest)


def setup_inputs(seed: int = 0) -> dict:
    arg_keys = jax.random.split(jax.random.key(seed), 5)
    return {
        "records": draw_records(jax.random.fold_in(arg_keys[4], 71), 0),
        "offsets": touch_ends(jax.random.randint(arg_keys[1], (NBLOCKS,), 0, BLOCK - BAND + 1), jax.random.fold_in(arg_keys[1], 1), 0, BLOCK - BAND).astype(jnp.int32),
        "column_map": jax.random.permutation(arg_keys[2], COLS).astype(jnp.int32),
        "angles": jnp.clip(jax.random.uniform(arg_keys[3], (GAUGES,), jnp.float32, -3.140625, 3.140625), -3.140625, 3.140625),
    }


def band_mask(offsets_here, total_rows):
    positions = jnp.arange(total_rows, dtype=jnp.int32)
    block_of = positions // BLOCK
    within = positions % BLOCK
    blocks = jnp.arange(offsets_here.shape[0], dtype=jnp.int32)
    inside = (block_of[None, :] == blocks[:, None]) & (within[None, :] >= offsets_here[:, None]) & (within[None, :] < offsets_here[:, None] + BAND)
    return inside.astype(jnp.bfloat16)

def drift_filter(rows, offsets_here):
    masks = band_mask(offsets_here, rows.shape[0])
    baseline = jnp.dot(masks.astype(jnp.float32), rows.astype(jnp.float32), preferred_element_type=jnp.float32) / BAND
    nblocks = offsets_here.shape[0]
    shaped = rows.astype(jnp.float32).reshape(nblocks, BLOCK, rows.shape[1]) - baseline[:, None, :]
    return shaped.reshape(rows.shape[0], rows.shape[1]).astype(jnp.bfloat16)

def rosette_rotate(full_rows, column_map, angles):
    count = angles.shape[0]
    picked = jnp.take(full_rows, column_map, axis=1)
    first_arm = picked[:, :count].astype(jnp.float32)
    middle_arm = picked[:, count:2 * count].astype(jnp.float32)
    last_arm = picked[:, 2 * count:].astype(jnp.float32)
    shear = 2.0 * middle_arm - first_arm - last_arm
    cosine = jnp.cos(angles)[None, :]
    sine = jnp.sin(angles)[None, :]
    cos_sq = cosine * cosine
    sin_sq = sine * sine
    mixed = sine * cosine
    along_x = first_arm * cos_sq + last_arm * sin_sq + shear * mixed
    along_y = first_arm * sin_sq + last_arm * cos_sq - shear * mixed
    shear_new = 2.0 * (last_arm - first_arm) * mixed + shear * (cos_sq - sin_sq)
    return jnp.concatenate([along_x, along_y, shear_new], axis=1).astype(jnp.bfloat16)

def gram_of(rotated):
    return lax.dot_general(rotated.astype(jnp.float32), rotated.astype(jnp.float32), (((0,), (0,)), ((), ())), preferred_element_type=jnp.float32)

def reference(records, offsets, column_map, angles):
    blocks = records.reshape(NBLOCKS, BLOCK, COLS)

    def accumulate(total, item):
        rows, offset_one = item
        filtered = drift_filter(rows, offset_one[None])
        rotated = rosette_rotate(filtered, column_map, angles)
        return (total + gram_of(rotated), None)
    total, unused = lax.scan(accumulate, jnp.zeros((COLS, COLS), jnp.float32), (blocks, offsets))
    return jnp.linalg.cholesky(total / SAMPLES).T
```

```python
import functools

import jax
import jax.numpy as jnp
from jax import lax
from jax.experimental import pallas as pl
from jax.experimental.pallas import tpu as pltpu
from jax.sharding import PartitionSpec as P

BLOCK = 1024
BAND = 64


def band_mask(offsets_here, total_rows):
    positions = jnp.arange(total_rows, dtype=jnp.int32)
    block_of = positions // BLOCK
    within = positions % BLOCK
    blocks = jnp.arange(offsets_here.shape[0], dtype=jnp.int32)
    inside = (
        (block_of[None, :] == blocks[:, None])
        & (within[None, :] >= offsets_here[:, None])
        & (within[None, :] < offsets_here[:, None] + BAND)
    )
    return inside.astype(jnp.bfloat16)


def drift_filter(rows, offsets_here):
    masks = band_mask(offsets_here, rows.shape[0])
    baseline = jnp.dot(masks, rows, preferred_element_type=jnp.float32) / BAND
    nblocks = offsets_here.shape[0]
    shaped = rows.astype(jnp.float32).reshape(nblocks, BLOCK, rows.shape[1]) - baseline[:, None, :]
    return shaped.reshape(rows.shape[0], rows.shape[1]).astype(jnp.bfloat16)


def rosette_rotate(full_rows, column_map, angles):
    count = angles.shape[0]
    picked = jnp.take(full_rows, column_map, axis=1)
    first_arm = picked[:, :count].astype(jnp.float32)
    middle_arm = picked[:, count : 2 * count].astype(jnp.float32)
    last_arm = picked[:, 2 * count :].astype(jnp.float32)
    shear = 2.0 * middle_arm - first_arm - last_arm
    cosine = jnp.cos(angles)[None, :]
    sine = jnp.sin(angles)[None, :]
    cos_sq = cosine * cosine
    sin_sq = sine * sine
    mixed = sine * cosine
    along_x = first_arm * cos_sq + last_arm * sin_sq + shear * mixed
    along_y = first_arm * sin_sq + last_arm * cos_sq - shear * mixed
    shear_new = 2.0 * (last_arm - first_arm) * mixed + shear * (cos_sq - sin_sq)
    return jnp.concatenate([along_x, along_y, shear_new], axis=1).astype(jnp.bfloat16)


N = 1536
NB = 128
TB = 384


def factor_tile(state):
    lane = lax.broadcasted_iota(jnp.int32, (8, NB), 1)
    sub = lax.broadcasted_iota(jnp.int32, (8, NB), 0)
    upper, inverse = [], []
    for s in range(NB // 8):
        base = 8 * s
        rows = state[s]
        here = (lane >= base) & (lane < base + 8)
        cols = [jnp.broadcast_to(rows[:, base + k : base + k + 1], (8, NB)) for k in range(8)]
        fwd = rows
        merged = jnp.where(here, (lane - base == sub).astype(jnp.float32), rows)
        fwd_inv = merged
        jordan = merged
        pivots = cols[0]
        for j in range(8):
            pivot = jnp.broadcast_to(cols[j][j : j + 1, :], (8, NB))
            pivots = jnp.where(sub == j, pivot, pivots)
            scaled = cols[j] * (1.0 / pivot)
            both = jnp.where(sub == j, 0.0, scaled)
            for k in range(j + 1, 8):
                cols[k] = cols[k] - both * jnp.broadcast_to(cols[k][j : j + 1, :], (8, NB))
            below = jnp.where(sub > j, scaled, 0.0)
            fwd = fwd - below * jnp.broadcast_to(fwd[j : j + 1, :], (8, NB))
            fwd_inv = fwd_inv - below * jnp.broadcast_to(fwd_inv[j : j + 1, :], (8, NB))
            jordan = jordan - both * jnp.broadcast_to(jordan[j : j + 1, :], (8, NB))
        root = lax.rsqrt(pivots)
        root = root * (1.5 - 0.5 * pivots * root * root)
        upper.append(jnp.where(lane >= sub + base, fwd * root, 0.0))
        inverse.append(jnp.where(lane <= sub + base, fwd_inv * root, 0.0))
        solved = jordan * (root * root)
        solved_rows = [jnp.broadcast_to(solved[k : k + 1, :], (8, NB)) for k in range(8)]
        for r in range(s + 1, NB // 8):
            old = state[r]
            new = jnp.where(here, 0.0, old)
            for k in range(8):
                new = new - jnp.broadcast_to(old[:, base + k : base + k + 1], (8, NB)) * solved_rows[k]
            state[r] = new
    return upper, inverse


def cholesky_kernel(scale, *refs):
    strips = refs[: N // TB]
    a_ref, inv_ref, left_ref, right_ref = refs[N // TB :]
    for i, strip in enumerate(strips):
        a_ref[i * TB : (i + 1) * TB, i * TB :] = strip[...] * scale
        if i > 0:
            a_ref[i * TB : (i + 1) * TB, : i * TB] = jnp.zeros((TB, i * TB), jnp.float32)

    def panel(k, carry):
        top = pl.multiple_of(k * NB, NB)
        rows = pl.ds(top, NB)
        state = [a_ref[pl.ds(top + 8 * s, 8), pl.ds(top, NB)] for s in range(NB // 8)]
        upper, inverse = factor_tile(state)
        for s in range(NB // 8):
            inv_ref[8 * s : 8 * s + 8, :] = inverse[s]
        solved = jnp.dot(
            inv_ref[...], a_ref[rows, :], precision=lax.Precision.HIGHEST, preferred_element_type=jnp.float32
        )
        col = lax.broadcasted_iota(jnp.int32, (NB, N), 1)
        solved = jnp.where(col >= top + NB, solved, 0.0)
        a_ref[rows, :] = solved
        for s in range(NB // 8):
            a_ref[pl.ds(top + 8 * s, 8), pl.ds(top, NB)] = upper[s]
        high = solved.astype(jnp.bfloat16)
        low = (solved - high.astype(jnp.float32)).astype(jnp.bfloat16)
        right_ref[0:NB, :] = high
        right_ref[NB : 2 * NB, :] = low
        right_ref[2 * NB : 3 * NB, :] = high
        right_ref[3 * NB : 4 * NB, :] = low
        first = (k + 1) // (TB // NB)

        def turn(i, carry):
            at = pl.multiple_of(i * TB, TB)
            turned = jnp.where(
                lax.broadcasted_iota(jnp.int32, (NB, TB), 1) + at >= top + NB, a_ref[rows, pl.ds(at, TB)], 0.0
            ).T
            high = turned.astype(jnp.bfloat16)
            low = (turned - high.astype(jnp.float32)).astype(jnp.bfloat16)
            left_ref[pl.ds(at, TB), 0:NB] = high
            left_ref[pl.ds(at, TB), NB : 2 * NB] = high
            left_ref[pl.ds(at, TB), 2 * NB : 3 * NB] = low
            left_ref[pl.ds(at, TB), 3 * NB : 4 * NB] = low
            return carry

        def update_row(i, carry):
            at = pl.multiple_of(i * TB, TB)

            def update(j, carry):
                to = pl.multiple_of(j * TB, TB)
                block = (pl.ds(at, TB), pl.ds(to, TB))
                a_ref[block] -= jnp.dot(
                    left_ref[pl.ds(at, TB), :], right_ref[:, pl.ds(to, TB)], preferred_element_type=jnp.float32
                )
                return carry

            return lax.fori_loop(i, N // TB, update, carry)

        @pl.when(k < N // NB - 1)
        def _():
            lax.fori_loop(first, N // TB, turn, 0)
            lax.fori_loop(first, N // TB, update_row, 0)

        return carry

    lax.fori_loop(0, N // NB, panel, 0)


def factor_of(strips, scale):
    return pl.pallas_call(
        functools.partial(cholesky_kernel, scale),
        out_shape=jax.ShapeDtypeStruct((N, N), jnp.float32),
        in_specs=[pl.BlockSpec(memory_space=pltpu.VMEM)] * len(strips),
        out_specs=pl.BlockSpec(memory_space=pltpu.VMEM),
        scratch_shapes=[
            pltpu.VMEM((NB, NB), jnp.float32),
            pltpu.VMEM((N, 4 * NB), jnp.bfloat16),
            pltpu.VMEM((4 * NB, N), jnp.bfloat16),
        ],
        compiler_params=pltpu.CompilerParams(vmem_limit_bytes=48 * 1024 * 1024),
        cost_estimate=pl.CostEstimate(flops=8 * N * N * N // 3, bytes_accessed=8 * N * N, transcendentals=0),
    )(*strips)


def gram_strips(rotated):
    return [
        lax.dot_general(
            rotated[:, at : at + TB],
            rotated[:, at:],
            (((0,), (0,)), ((), ())),
            preferred_element_type=jnp.float32,
        )
        for at in range(0, N, TB)
    ]


def shards(records, offsets, column_map, angles):
    filtered = drift_filter(records, offsets)
    regrouped = lax.all_to_all(filtered, "gauge", split_axis=0, concat_axis=1, tiled=True)
    rotated = rosette_rotate(regrouped, column_map, angles)
    total_rows = rotated.shape[0] * lax.axis_size("tm") * lax.axis_size("gauge")
    strips = [lax.psum(strip, ("tm", "gauge")) for strip in gram_strips(rotated)]
    return factor_of(strips, 1.0 / total_rows)


def solution(mesh):
    placed = (P("tm", "gauge"), P("tm"), P(), P())
    return jax.shard_map(shards, mesh=mesh, in_specs=placed, out_specs=P(), check_vma=False)
```

```python
import functools

import jax
import jax.numpy as jnp
from jax import lax
from jax.experimental import pallas as pl
from jax.experimental.pallas import tpu as pltpu
from jax.sharding import PartitionSpec as P

BLOCK = 1024
BAND = 64


def band_mask(offsets_here, total_rows):
    positions = jnp.arange(total_rows, dtype=jnp.int32)
    block_of = positions // BLOCK
    within = positions % BLOCK
    blocks = jnp.arange(offsets_here.shape[0], dtype=jnp.int32)
    inside = (
        (block_of[None, :] == blocks[:, None])
        & (within[None, :] >= offsets_here[:, None])
        & (within[None, :] < offsets_here[:, None] + BAND)
    )
    return inside.astype(jnp.bfloat16)


def drift_filter(rows, offsets_here):
    masks = band_mask(offsets_here, rows.shape[0])
    baseline = jnp.dot(masks, rows, preferred_element_type=jnp.float32) / BAND
    nblocks = offsets_here.shape[0]
    shaped = rows.astype(jnp.float32).reshape(nblocks, BLOCK, rows.shape[1]) - baseline[:, None, :]
    return shaped.reshape(rows.shape[0], rows.shape[1]).astype(jnp.bfloat16)


def rosette_rotate(full_rows, column_map, angles):
    count = angles.shape[0]
    picked = jnp.take(full_rows, column_map, axis=1)
    first_arm = picked[:, :count].astype(jnp.float32)
    middle_arm = picked[:, count : 2 * count].astype(jnp.float32)
    last_arm = picked[:, 2 * count :].astype(jnp.float32)
    shear = 2.0 * middle_arm - first_arm - last_arm
    cosine = jnp.cos(angles)[None, :]
    sine = jnp.sin(angles)[None, :]
    cos_sq = cosine * cosine
    sin_sq = sine * sine
    mixed = sine * cosine
    along_x = first_arm * cos_sq + last_arm * sin_sq + shear * mixed
    along_y = first_arm * sin_sq + last_arm * cos_sq - shear * mixed
    shear_new = 2.0 * (last_arm - first_arm) * mixed + shear * (cos_sq - sin_sq)
    return jnp.concatenate([along_x, along_y, shear_new], axis=1).astype(jnp.bfloat16)


N = 1536
NB = 128
TB = 384


TILES = [(i, j) for i in range(N // NB) for j in range(i, N // NB)]
MESH = pl.DeviceIdType.MESH


def sum_kernel(sizes, *refs):
    strips = refs[: N // TB]
    out_ref, acc_ref, land_ref, rs_send, rs_recv, ag_send, ag_recv = refs[N // TB :]
    size_z, size_x, size_y = sizes
    tm, gauge = lax.axis_index("tm"), lax.axis_index("gauge")
    at = {
        "z": lax.div(tm, size_x),
        "x": lax.rem(tm, size_x),
        "y": lax.div(gauge, 2),
        "core": lax.rem(gauge, 2),
    }
    size = {"z": size_z, "x": size_x, "y": size_y, "core": 2}

    def peer(axis, d):
        there = dict(at)
        there[axis] = lax.rem(at[axis] + d, size[axis])
        return there[axis], (there["z"] * size_x + there["x"], there["y"] * 2 + there["core"])

    barrier = pltpu.get_barrier_semaphore()
    friends = [peer(axis, d)[1] for axis in size for d in range(1, size[axis])]
    for friend in friends:
        pl.semaphore_signal(barrier, inc=1, device_id=friend, device_id_type=MESH)

    for t, (i, j) in enumerate(TILES):
        s = i * NB // TB
        acc_ref[t * NB : (t + 1) * NB, :] = strips[s][
            i * NB - s * TB : (i + 1) * NB - s * TB, j * NB - s * TB : (j + 1) * NB - s * TB
        ]
    total = acc_ref.shape[0]
    filled = len(TILES) * NB
    if filled < total:
        acc_ref[filled:, :] = jnp.zeros((total - filled, NB), jnp.float32)

    pl.semaphore_wait(barrier, len(friends))

    orders = [("core", "y", "x", "z"), ("core", "x", "y", "z")]
    base = [p * (total // 2) for p in range(2)]
    length = [total // 2] * 2
    slots = [0, 0]
    marks = [[], []]

    def scatter_start(p, stage):
        axis = orders[p][stage]
        n = size[axis]
        piece = length[p] // n
        copies = []
        for d in range(1, n):
            index, device = peer(axis, d)
            slot = slots[p]
            slots[p] += 1
            land = land_ref.at[p, pl.ds(lands[p], piece), :]
            copy = pltpu.make_async_remote_copy(
                src_ref=acc_ref.at[pl.ds(pl.multiple_of(base[p] + index * piece, 8), piece), :],
                dst_ref=land,
                send_sem=rs_send.at[p, slot],
                recv_sem=rs_recv.at[p, slot],
                device_id=device,
                device_id_type=MESH,
            )
            copy.start()
            copies.append((copy, lands[p]))
            lands[p] += piece
        return copies, piece, axis

    def scatter_finish(p, started):
        copies, piece, axis = started
        marks[p].append((base[p], length[p], axis))
        base[p] = pl.multiple_of(base[p] + at[axis] * piece, 8)
        length[p] = piece
        rows = pl.ds(base[p], piece)
        value = acc_ref[rows, :]
        for copy, where in copies:
            copy.wait_recv()
            value = value + land_ref[p, where : where + piece, :]
        if len(marks[p]) < 4:
            acc_ref[rows, :] = value
        else:
            out_ref[rows, :] = value
        sent.extend(copy for copy, where in copies)

    def gather_start(p):
        whole_base, whole_length, axis = marks[p][-1]
        rows = pl.ds(base[p], length[p])
        copies = []
        for d in range(1, size[axis]):
            index, device = peer(axis, d)
            slot = slots[p]
            slots[p] += 1
            copy = pltpu.make_async_remote_copy(
                src_ref=out_ref.at[rows, :],
                dst_ref=out_ref.at[rows, :],
                send_sem=ag_send.at[p, slot],
                recv_sem=ag_recv.at[p, slot],
                device_id=device,
                device_id_type=MESH,
            )
            copy.start()
            copies.append(copy)
        return copies

    def gather_finish(p, copies):
        for copy in copies:
            copy.wait_recv()
        sent.extend(copies)
        base[p], length[p], axis = marks[p].pop()

    sent = []
    lands = [0, 0]
    flying = [scatter_start(p, 0) for p in range(2)]
    for stage in range(4):
        for p in range(2):
            scatter_finish(p, flying[p])
            if stage < 3:
                flying[p] = scatter_start(p, stage + 1)
            else:
                slots[p] = 0
                flying[p] = gather_start(p)
    for stage in range(4):
        for p in range(2):
            gather_finish(p, flying[p])
            if stage < 3:
                flying[p] = gather_start(p)
    for copy in sent:
        copy.wait_send()


def summed(strips, sizes):
    size_z, size_x, size_y = sizes
    unit = 4 * 8 * size_z * size_x * size_y
    total = -(-len(TILES) * NB // unit) * unit
    sends = size_z + size_x + size_y - 2
    length = total // 2
    landing = 0
    for n in (2, size_x, size_y, size_z):
        landing += length // n * (n - 1)
        length //= n
    return pl.pallas_call(
        functools.partial(sum_kernel, sizes),
        out_shape=jax.ShapeDtypeStruct((total, NB), jnp.float32),
        in_specs=[pl.BlockSpec(memory_space=pltpu.VMEM)] * len(strips),
        out_specs=pl.BlockSpec(memory_space=pltpu.VMEM),
        scratch_shapes=[
            pltpu.VMEM((total, NB), jnp.float32),
            pltpu.VMEM((2, landing, NB), jnp.float32),
            pltpu.SemaphoreType.DMA((2, sends)),
            pltpu.SemaphoreType.DMA((2, sends)),
            pltpu.SemaphoreType.DMA((2, sends)),
            pltpu.SemaphoreType.DMA((2, sends)),
        ],
        compiler_params=pltpu.CompilerParams(
            collective_id=0, has_side_effects=True, vmem_limit_bytes=48 * 1024 * 1024
        ),
        cost_estimate=pl.CostEstimate(flops=total * NB, bytes_accessed=16 * total * NB, transcendentals=0),
    )(*strips)


def factor_tile(state):
    lane = lax.broadcasted_iota(jnp.int32, (8, NB), 1)
    sub = lax.broadcasted_iota(jnp.int32, (8, NB), 0)
    upper, inverse = [], []
    for s in range(NB // 8):
        base = 8 * s
        rows = state[s]
        here = (lane >= base) & (lane < base + 8)
        cols = [jnp.broadcast_to(rows[:, base + k : base + k + 1], (8, NB)) for k in range(8)]
        fwd = rows
        merged = jnp.where(here, (lane - base == sub).astype(jnp.float32), rows)
        fwd_inv = merged
        jordan = merged
        pivots = cols[0]
        for j in range(8):
            pivot = jnp.broadcast_to(cols[j][j : j + 1, :], (8, NB))
            pivots = jnp.where(sub == j, pivot, pivots)
            scaled = cols[j] * (1.0 / pivot)
            both = jnp.where(sub == j, 0.0, scaled)
            for k in range(j + 1, 8):
                cols[k] = cols[k] - both * jnp.broadcast_to(cols[k][j : j + 1, :], (8, NB))
            below = jnp.where(sub > j, scaled, 0.0)
            fwd = fwd - below * jnp.broadcast_to(fwd[j : j + 1, :], (8, NB))
            fwd_inv = fwd_inv - below * jnp.broadcast_to(fwd_inv[j : j + 1, :], (8, NB))
            jordan = jordan - both * jnp.broadcast_to(jordan[j : j + 1, :], (8, NB))
        root = lax.rsqrt(pivots)
        root = root * (1.5 - 0.5 * pivots * root * root)
        upper.append(jnp.where(lane >= sub + base, fwd * root, 0.0))
        inverse.append(jnp.where(lane <= sub + base, fwd_inv * root, 0.0))
        solved = jordan * (root * root)
        solved_rows = [jnp.broadcast_to(solved[k : k + 1, :], (8, NB)) for k in range(8)]
        for r in range(s + 1, NB // 8):
            old = state[r]
            new = jnp.where(here, 0.0, old)
            for k in range(8):
                new = new - jnp.broadcast_to(old[:, base + k : base + k + 1], (8, NB)) * solved_rows[k]
            state[r] = new
    return upper, inverse


def cholesky_kernel(scale, *refs):
    packed_ref, a_ref, inv_ref, left_ref, right_ref = refs
    a_ref[...] = jnp.zeros_like(a_ref)
    for t, (i, j) in enumerate(TILES):
        a_ref[i * NB : (i + 1) * NB, j * NB : (j + 1) * NB] = packed_ref[t * NB : (t + 1) * NB, :] * scale

    def panel(k, carry):
        top = pl.multiple_of(k * NB, NB)
        rows = pl.ds(top, NB)
        state = [a_ref[pl.ds(top + 8 * s, 8), pl.ds(top, NB)] for s in range(NB // 8)]
        upper, inverse = factor_tile(state)
        for s in range(NB // 8):
            inv_ref[8 * s : 8 * s + 8, :] = inverse[s]
        solved = jnp.dot(
            inv_ref[...], a_ref[rows, :], precision=lax.Precision.HIGHEST, preferred_element_type=jnp.float32
        )
        col = lax.broadcasted_iota(jnp.int32, (NB, N), 1)
        solved = jnp.where(col >= top + NB, solved, 0.0)
        a_ref[rows, :] = solved
        for s in range(NB // 8):
            a_ref[pl.ds(top + 8 * s, 8), pl.ds(top, NB)] = upper[s]
        high = solved.astype(jnp.bfloat16)
        low = (solved - high.astype(jnp.float32)).astype(jnp.bfloat16)
        right_ref[0:NB, :] = high
        right_ref[NB : 2 * NB, :] = low
        right_ref[2 * NB : 3 * NB, :] = high
        right_ref[3 * NB : 4 * NB, :] = low
        first = (k + 1) // (TB // NB)

        def turn(i, carry):
            at = pl.multiple_of(i * TB, TB)
            turned = jnp.where(
                lax.broadcasted_iota(jnp.int32, (NB, TB), 1) + at >= top + NB, a_ref[rows, pl.ds(at, TB)], 0.0
            ).T
            high = turned.astype(jnp.bfloat16)
            low = (turned - high.astype(jnp.float32)).astype(jnp.bfloat16)
            left_ref[pl.ds(at, TB), 0:NB] = high
            left_ref[pl.ds(at, TB), NB : 2 * NB] = high
            left_ref[pl.ds(at, TB), 2 * NB : 3 * NB] = low
            left_ref[pl.ds(at, TB), 3 * NB : 4 * NB] = low
            return carry

        def update_row(i, carry):
            at = pl.multiple_of(i * TB, TB)

            def update(j, carry):
                to = pl.multiple_of(j * TB, TB)
                block = (pl.ds(at, TB), pl.ds(to, TB))
                a_ref[block] -= jnp.dot(
                    left_ref[pl.ds(at, TB), :], right_ref[:, pl.ds(to, TB)], preferred_element_type=jnp.float32
                )
                return carry

            return lax.fori_loop(i, N // TB, update, carry)

        @pl.when(k < N // NB - 1)
        def _():
            lax.fori_loop(first, N // TB, turn, 0)
            lax.fori_loop(first, N // TB, update_row, 0)

        return carry

    lax.fori_loop(0, N // NB, panel, 0)


def factor_of(packed, scale):
    return pl.pallas_call(
        functools.partial(cholesky_kernel, scale),
        out_shape=jax.ShapeDtypeStruct((N, N), jnp.float32),
        in_specs=[pl.BlockSpec(memory_space=pltpu.VMEM)],
        out_specs=pl.BlockSpec(memory_space=pltpu.VMEM),
        scratch_shapes=[
            pltpu.VMEM((NB, NB), jnp.float32),
            pltpu.VMEM((N, 4 * NB), jnp.bfloat16),
            pltpu.VMEM((4 * NB, N), jnp.bfloat16),
        ],
        compiler_params=pltpu.CompilerParams(vmem_limit_bytes=48 * 1024 * 1024),
        cost_estimate=pl.CostEstimate(flops=8 * N * N * N // 3, bytes_accessed=8 * N * N, transcendentals=0),
    )(packed)


def gram_strips(rotated):
    return [
        lax.dot_general(
            rotated[:, at : at + TB],
            rotated[:, at:],
            (((0,), (0,)), ((), ())),
            preferred_element_type=jnp.float32,
        )
        for at in range(0, N, TB)
    ]


PARTS = 2


def shards(records, offsets, column_map, angles):
    total_rows = records.shape[0] * lax.axis_size("tm")
    rows = records.shape[0] // PARTS
    blocks = offsets.shape[0] // PARTS
    strips = None
    for part in range(PARTS):
        filtered = drift_filter(
            records[part * rows : (part + 1) * rows], offsets[part * blocks : (part + 1) * blocks]
        )
        regrouped = lax.all_to_all(filtered, "gauge", split_axis=0, concat_axis=1, tiled=True)
        rotated = rosette_rotate(regrouped, column_map, angles)
        terms = gram_strips(rotated)
        strips = terms if strips is None else [one + other for one, other in zip(strips, terms)]
    size_y = lax.axis_size("gauge") // 2
    sizes = (lax.axis_size("tm") // size_y, size_y, size_y)
    return factor_of(summed(strips, sizes), 1.0 / total_rows)


def solution(mesh):
    placed = (P("tm", "gauge"), P("tm"), P(), P())
    return jax.shard_map(shards, mesh=mesh, in_specs=placed, out_specs=P(), check_vma=False)
```

```python
import functools

import jax
import jax.numpy as jnp
from jax import lax
from jax.experimental import pallas as pl
from jax.experimental.pallas import tpu as pltpu
from jax.sharding import PartitionSpec as P

BLOCK = 1024
BAND = 64


def band_mask(offsets_here, total_rows):
    positions = jnp.arange(total_rows, dtype=jnp.int32)
    block_of = positions // BLOCK
    within = positions % BLOCK
    blocks = jnp.arange(offsets_here.shape[0], dtype=jnp.int32)
    inside = (
        (block_of[None, :] == blocks[:, None])
        & (within[None, :] >= offsets_here[:, None])
        & (within[None, :] < offsets_here[:, None] + BAND)
    )
    return inside.astype(jnp.bfloat16)


def drift_filter(rows, offsets_here):
    masks = band_mask(offsets_here, rows.shape[0])
    baseline = jnp.dot(masks, rows, preferred_element_type=jnp.float32) / BAND
    nblocks = offsets_here.shape[0]
    shaped = rows.astype(jnp.float32).reshape(nblocks, BLOCK, rows.shape[1]) - baseline[:, None, :]
    return shaped.reshape(rows.shape[0], rows.shape[1]).astype(jnp.bfloat16)


def rosette_rotate(full_rows, column_map, angles):
    count = angles.shape[0]
    picked = jnp.take(full_rows, column_map, axis=1)
    first_arm = picked[:, :count].astype(jnp.float32)
    middle_arm = picked[:, count : 2 * count].astype(jnp.float32)
    last_arm = picked[:, 2 * count :].astype(jnp.float32)
    shear = 2.0 * middle_arm - first_arm - last_arm
    cosine = jnp.cos(angles)[None, :]
    sine = jnp.sin(angles)[None, :]
    cos_sq = cosine * cosine
    sin_sq = sine * sine
    mixed = sine * cosine
    along_x = first_arm * cos_sq + last_arm * sin_sq + shear * mixed
    along_y = first_arm * sin_sq + last_arm * cos_sq - shear * mixed
    shear_new = 2.0 * (last_arm - first_arm) * mixed + shear * (cos_sq - sin_sq)
    return jnp.concatenate([along_x, along_y, shear_new], axis=1).astype(jnp.bfloat16)


N = 1536
NB = 128
TB = 384


TILES = [(i, j) for i in range(N // NB) for j in range(i, N // NB)]
MESH = pl.DeviceIdType.MESH
PIECES = 4


def sum_kernel(sizes, *refs):
    strips = refs[: N // TB]
    out_ref, acc_ref, land_ref, rs_send, rs_recv, ag_send, ag_recv = refs[N // TB :]
    size_z, size_x, size_y = sizes
    tm, gauge = lax.axis_index("tm"), lax.axis_index("gauge")
    at = {
        "z": lax.div(tm, size_x),
        "x": lax.rem(tm, size_x),
        "y": lax.div(gauge, 2),
        "core": lax.rem(gauge, 2),
    }
    size = {"z": size_z, "x": size_x, "y": size_y, "core": 2}

    def peer(axis, d):
        there = dict(at)
        there[axis] = lax.rem(at[axis] + d, size[axis])
        return there[axis], (there["z"] * size_x + there["x"], there["y"] * 2 + there["core"])

    barrier = pltpu.get_barrier_semaphore()
    friends = [peer(axis, d)[1] for axis in size for d in range(1, size[axis])]
    for friend in friends:
        pl.semaphore_signal(barrier, inc=1, device_id=friend, device_id_type=MESH)

    for t, (i, j) in enumerate(TILES):
        s = i * NB // TB
        acc_ref[t * NB : (t + 1) * NB, :] = strips[s][
            i * NB - s * TB : (i + 1) * NB - s * TB, j * NB - s * TB : (j + 1) * NB - s * TB
        ]
    total = acc_ref.shape[0]
    filled = len(TILES) * NB
    if filled < total:
        acc_ref[filled:, :] = jnp.zeros((total - filled, NB), jnp.float32)

    pl.semaphore_wait(barrier, len(friends))

    orders = [("core", "y", "x", "z"), ("core", "x", "y", "z")] * (PIECES // 2)
    base = [p * (total // PIECES) for p in range(PIECES)]
    length = [total // PIECES] * PIECES
    slots = [0] * PIECES
    marks = [[] for p in range(PIECES)]

    def scatter_start(p, stage):
        axis = orders[p][stage]
        n = size[axis]
        piece = length[p] // n
        copies = []
        for d in range(1, n):
            index, device = peer(axis, d)
            slot = slots[p]
            slots[p] += 1
            land = land_ref.at[p, pl.ds(lands[p], piece), :]
            copy = pltpu.make_async_remote_copy(
                src_ref=acc_ref.at[pl.ds(pl.multiple_of(base[p] + index * piece, 8), piece), :],
                dst_ref=land,
                send_sem=rs_send.at[p, slot],
                recv_sem=rs_recv.at[p, slot],
                device_id=device,
                device_id_type=MESH,
            )
            copy.start()
            copies.append((copy, lands[p]))
            lands[p] += piece
        return copies, piece, axis

    def scatter_finish(p, started):
        copies, piece, axis = started
        marks[p].append((base[p], length[p], axis))
        base[p] = pl.multiple_of(base[p] + at[axis] * piece, 8)
        length[p] = piece
        rows = pl.ds(base[p], piece)
        value = acc_ref[rows, :]
        for copy, where in copies:
            copy.wait_recv()
            value = value + land_ref[p, where : where + piece, :]
        if len(marks[p]) < 4:
            acc_ref[rows, :] = value
        else:
            out_ref[rows, :] = value
        sent.extend(copy for copy, where in copies)

    def gather_start(p):
        whole_base, whole_length, axis = marks[p][-1]
        rows = pl.ds(base[p], length[p])
        copies = []
        for d in range(1, size[axis]):
            index, device = peer(axis, d)
            slot = slots[p]
            slots[p] += 1
            copy = pltpu.make_async_remote_copy(
                src_ref=out_ref.at[rows, :],
                dst_ref=out_ref.at[rows, :],
                send_sem=ag_send.at[p, slot],
                recv_sem=ag_recv.at[p, slot],
                device_id=device,
                device_id_type=MESH,
            )
            copy.start()
            copies.append(copy)
        return copies

    def gather_finish(p, copies):
        for copy in copies:
            copy.wait_recv()
        sent.extend(copies)
        base[p], length[p], axis = marks[p].pop()

    sent = []
    lands = [0] * PIECES
    flying = [scatter_start(p, 0) for p in range(PIECES)]
    for stage in range(4):
        for p in range(PIECES):
            scatter_finish(p, flying[p])
            if stage < 3:
                flying[p] = scatter_start(p, stage + 1)
            else:
                slots[p] = 0
                flying[p] = gather_start(p)
    for stage in range(4):
        for p in range(PIECES):
            gather_finish(p, flying[p])
            if stage < 3:
                flying[p] = gather_start(p)
    for copy in sent:
        copy.wait_send()


def summed(strips, sizes):
    size_z, size_x, size_y = sizes
    unit = 2 * PIECES * 8 * size_z * size_x * size_y
    total = -(-len(TILES) * NB // unit) * unit
    sends = size_z + size_x + size_y - 2
    length = total // PIECES
    landing = 0
    for n in (2, size_x, size_y, size_z):
        landing += length // n * (n - 1)
        length //= n
    return pl.pallas_call(
        functools.partial(sum_kernel, sizes),
        out_shape=jax.ShapeDtypeStruct((total, NB), jnp.float32),
        in_specs=[pl.BlockSpec(memory_space=pltpu.VMEM)] * len(strips),
        out_specs=pl.BlockSpec(memory_space=pltpu.VMEM),
        scratch_shapes=[
            pltpu.VMEM((total, NB), jnp.float32),
            pltpu.VMEM((PIECES, landing, NB), jnp.float32),
            pltpu.SemaphoreType.DMA((PIECES, sends)),
            pltpu.SemaphoreType.DMA((PIECES, sends)),
            pltpu.SemaphoreType.DMA((PIECES, sends)),
            pltpu.SemaphoreType.DMA((PIECES, sends)),
        ],
        compiler_params=pltpu.CompilerParams(
            collective_id=0, has_side_effects=True, vmem_limit_bytes=48 * 1024 * 1024
        ),
        cost_estimate=pl.CostEstimate(flops=total * NB, bytes_accessed=16 * total * NB, transcendentals=0),
    )(*strips)


def factor_tile(state):
    lane = lax.broadcasted_iota(jnp.int32, (8, NB), 1)
    sub = lax.broadcasted_iota(jnp.int32, (8, NB), 0)
    upper, inverse = [], []
    for s in range(NB // 8):
        base = 8 * s
        rows = state[s]
        here = (lane >= base) & (lane < base + 8)
        cols = [jnp.broadcast_to(rows[:, base + k : base + k + 1], (8, NB)) for k in range(8)]
        fwd = rows
        merged = jnp.where(here, (lane - base == sub).astype(jnp.float32), rows)
        fwd_inv = merged
        jordan = merged
        pivots = cols[0]
        pivot = jnp.broadcast_to(cols[0][0:1, :], (8, NB))
        for j in range(8):
            pivots = jnp.where(sub == j, pivot, pivots)
            reciprocal = 1.0 / pivot
            masked = jnp.where(sub == j, 0.0, cols[j])
            scaled = cols[j] * reciprocal
            both = masked * reciprocal
            if j < 7:
                corner = jnp.broadcast_to(cols[j + 1][j + 1 : j + 2, :], (8, NB))
                across = jnp.broadcast_to(cols[j + 1][j : j + 1, :], (8, NB))
                down = jnp.broadcast_to(cols[j][j + 1 : j + 2, :], (8, NB))
                pivot = corner - (down * across) * reciprocal
            for k in range(j + 1, 8):
                cols[k] = cols[k] - both * jnp.broadcast_to(cols[k][j : j + 1, :], (8, NB))
            below = jnp.where(sub > j, scaled, 0.0)
            fwd = fwd - below * jnp.broadcast_to(fwd[j : j + 1, :], (8, NB))
            fwd_inv = fwd_inv - below * jnp.broadcast_to(fwd_inv[j : j + 1, :], (8, NB))
            jordan = jordan - both * jnp.broadcast_to(jordan[j : j + 1, :], (8, NB))
        root = lax.rsqrt(pivots)
        root = root * (1.5 - 0.5 * pivots * root * root)
        upper.append(jnp.where(lane >= sub + base, fwd * root, 0.0))
        inverse.append(jnp.where(lane <= sub + base, fwd_inv * root, 0.0))
        solved = jordan * (root * root)
        solved_rows = [jnp.broadcast_to(solved[k : k + 1, :], (8, NB)) for k in range(8)]
        for r in range(s + 1, NB // 8):
            old = state[r]
            new = jnp.where(here, 0.0, old)
            for k in range(8):
                new = new - jnp.broadcast_to(old[:, base + k : base + k + 1], (8, NB)) * solved_rows[k]
            state[r] = new
    return upper, inverse


def cholesky_kernel(scale, *refs):
    packed_ref, a_ref, inv_ref, left_ref, right_ref = refs
    a_ref[...] = jnp.zeros_like(a_ref)
    for t, (i, j) in enumerate(TILES):
        a_ref[i * NB : (i + 1) * NB, j * NB : (j + 1) * NB] = packed_ref[t * NB : (t + 1) * NB, :] * scale

    def panel(k, carry):
        top = pl.multiple_of(k * NB, NB)
        rows = pl.ds(top, NB)
        state = [a_ref[pl.ds(top + 8 * s, 8), pl.ds(top, NB)] for s in range(NB // 8)]
        upper, inverse = factor_tile(state)
        for s in range(NB // 8):
            inv_ref[8 * s : 8 * s + 8, :] = inverse[s]
        def solve(i, carry):
            at = pl.multiple_of(i * TB, TB)
            part = pl.ds(at, TB)
            solved = jnp.dot(
                inv_ref[...], a_ref[rows, part], precision=lax.Precision.HIGHEST, preferred_element_type=jnp.float32
            )
            col = lax.broadcasted_iota(jnp.int32, (NB, TB), 1) + at
            solved = jnp.where(col >= top + NB, solved, 0.0)
            a_ref[rows, part] = solved
            high = solved.astype(jnp.bfloat16)
            low = (solved - high.astype(jnp.float32)).astype(jnp.bfloat16)
            right_ref[0:NB, part] = high
            right_ref[NB : 2 * NB, part] = low
            right_ref[2 * NB : 3 * NB, part] = high
            right_ref[3 * NB : 4 * NB, part] = low
            turned = solved.T
            high = turned.astype(jnp.bfloat16)
            low = (turned - high.astype(jnp.float32)).astype(jnp.bfloat16)
            left_ref[part, 0:NB] = high
            left_ref[part, NB : 2 * NB] = high
            left_ref[part, 2 * NB : 3 * NB] = low
            left_ref[part, 3 * NB : 4 * NB] = low
            return carry

        lax.fori_loop(k // (TB // NB), N // TB, solve, 0)
        for s in range(NB // 8):
            a_ref[pl.ds(top + 8 * s, 8), pl.ds(top, NB)] = upper[s]

        def update_row(i, carry):
            at = pl.multiple_of(i * TB, TB)

            def update(j, carry):
                to = pl.multiple_of(j * TB, TB)
                block = (pl.ds(at, TB), pl.ds(to, TB))
                a_ref[block] -= jnp.dot(
                    left_ref[pl.ds(at, TB), :], right_ref[:, pl.ds(to, TB)], preferred_element_type=jnp.float32
                )
                return carry

            return lax.fori_loop(i, N // TB, update, carry)

        return lax.fori_loop((k + 1) // (TB // NB), N // TB, update_row, carry)

    lax.fori_loop(0, N // NB, panel, 0)


def factor_of(packed, scale):
    return pl.pallas_call(
        functools.partial(cholesky_kernel, scale),
        out_shape=jax.ShapeDtypeStruct((N, N), jnp.float32),
        in_specs=[pl.BlockSpec(memory_space=pltpu.VMEM)],
        out_specs=pl.BlockSpec(memory_space=pltpu.VMEM),
        scratch_shapes=[
            pltpu.VMEM((NB, NB), jnp.float32),
            pltpu.VMEM((N, 4 * NB), jnp.bfloat16),
            pltpu.VMEM((4 * NB, N), jnp.bfloat16),
        ],
        compiler_params=pltpu.CompilerParams(vmem_limit_bytes=48 * 1024 * 1024),
        cost_estimate=pl.CostEstimate(flops=8 * N * N * N // 3, bytes_accessed=8 * N * N, transcendentals=0),
    )(packed)


def gram_strips(rotated):
    return [
        lax.dot_general(
            rotated[:, at : at + TB],
            rotated[:, at:],
            (((0,), (0,)), ((), ())),
            preferred_element_type=jnp.float32,
        )
        for at in range(0, N, TB)
    ]


PARTS = 2


def shards(records, offsets, column_map, angles):
    total_rows = records.shape[0] * lax.axis_size("tm")
    rows = records.shape[0] // PARTS
    blocks = offsets.shape[0] // PARTS
    strips = None
    for part in range(PARTS):
        filtered = drift_filter(
            records[part * rows : (part + 1) * rows], offsets[part * blocks : (part + 1) * blocks]
        )
        regrouped = lax.all_to_all(filtered, "gauge", split_axis=0, concat_axis=1, tiled=True)
        rotated = rosette_rotate(regrouped, column_map, angles)
        terms = gram_strips(rotated)
        strips = terms if strips is None else [one + other for one, other in zip(strips, terms)]
    size_y = lax.axis_size("gauge") // 2
    sizes = (lax.axis_size("tm") // size_y, size_y, size_y)
    return factor_of(summed(strips, sizes), 1.0 / total_rows)


def solution(mesh):
    placed = (P("tm", "gauge"), P("tm"), P(), P())
    return jax.shard_map(shards, mesh=mesh, in_specs=placed, out_specs=P(), check_vma=False)
```

```python
import functools

import jax
import jax.numpy as jnp
from jax import lax
from jax.experimental import pallas as pl
from jax.experimental.pallas import tpu as pltpu
from jax.sharding import PartitionSpec as P

BLOCK = 1024
BAND = 64


def band_mask(offsets_here, total_rows):
    positions = jnp.arange(total_rows, dtype=jnp.int32)
    block_of = positions // BLOCK
    within = positions % BLOCK
    blocks = jnp.arange(offsets_here.shape[0], dtype=jnp.int32)
    inside = (
        (block_of[None, :] == blocks[:, None])
        & (within[None, :] >= offsets_here[:, None])
        & (within[None, :] < offsets_here[:, None] + BAND)
    )
    return inside.astype(jnp.bfloat16)


def drift_filter(rows, offsets_here):
    masks = band_mask(offsets_here, rows.shape[0])
    baseline = jnp.dot(masks, rows, preferred_element_type=jnp.float32) / BAND
    nblocks = offsets_here.shape[0]
    shaped = rows.astype(jnp.float32).reshape(nblocks, BLOCK, rows.shape[1]) - baseline[:, None, :]
    return shaped.reshape(rows.shape[0], rows.shape[1]).astype(jnp.bfloat16)


def rosette_rotate(full_rows, column_map, angles):
    count = angles.shape[0]
    picked = jnp.take(full_rows, column_map, axis=1)
    first_arm = picked[:, :count].astype(jnp.float32)
    middle_arm = picked[:, count : 2 * count].astype(jnp.float32)
    last_arm = picked[:, 2 * count :].astype(jnp.float32)
    shear = 2.0 * middle_arm - first_arm - last_arm
    cosine = jnp.cos(angles)[None, :]
    sine = jnp.sin(angles)[None, :]
    cos_sq = cosine * cosine
    sin_sq = sine * sine
    mixed = sine * cosine
    along_x = first_arm * cos_sq + last_arm * sin_sq + shear * mixed
    along_y = first_arm * sin_sq + last_arm * cos_sq - shear * mixed
    shear_new = 2.0 * (last_arm - first_arm) * mixed + shear * (cos_sq - sin_sq)
    return jnp.concatenate([along_x, along_y, shear_new], axis=1).astype(jnp.bfloat16)


N = 1536
NB = 128
TB = 384


TILES = [(i, j) for i in range(N // NB) for j in range(i, N // NB)]
MESH = pl.DeviceIdType.MESH
PIECES = 8


def sum_kernel(sizes, *refs):
    strips = refs[: N // TB]
    out_ref, acc_ref, land_ref, rs_send, rs_recv, ag_send, ag_recv = refs[N // TB :]
    size_z, size_x, size_y = sizes
    tm, gauge = lax.axis_index("tm"), lax.axis_index("gauge")
    at = {
        "z": lax.div(tm, size_x),
        "x": lax.rem(tm, size_x),
        "y": lax.div(gauge, 2),
        "core": lax.rem(gauge, 2),
    }
    size = {"z": size_z, "x": size_x, "y": size_y, "core": 2}

    def peer(axis, d):
        there = dict(at)
        there[axis] = lax.rem(at[axis] + d, size[axis])
        return there[axis], (there["z"] * size_x + there["x"], there["y"] * 2 + there["core"])

    barrier = pltpu.get_barrier_semaphore()
    friends = [peer(axis, d)[1] for axis in size for d in range(1, size[axis])]
    for friend in friends:
        pl.semaphore_signal(barrier, inc=1, device_id=friend, device_id_type=MESH)

    for t, (i, j) in enumerate(TILES):
        s = i * NB // TB
        acc_ref[t * NB : (t + 1) * NB, :] = strips[s][
            i * NB - s * TB : (i + 1) * NB - s * TB, j * NB - s * TB : (j + 1) * NB - s * TB
        ]
    total = acc_ref.shape[0]
    filled = len(TILES) * NB
    if filled < total:
        acc_ref[filled:, :] = jnp.zeros((total - filled, NB), jnp.float32)

    pl.semaphore_wait(barrier, len(friends))

    orders = [("core", "y", "x", "z"), ("core", "x", "y", "z")] * (PIECES // 2)
    base = [p * (total // PIECES) for p in range(PIECES)]
    length = [total // PIECES] * PIECES
    slots = [0] * PIECES
    marks = [[] for p in range(PIECES)]

    def scatter_start(p, stage):
        axis = orders[p][stage]
        n = size[axis]
        piece = length[p] // n
        copies = []
        for d in range(1, n):
            index, device = peer(axis, d)
            slot = slots[p]
            slots[p] += 1
            land = land_ref.at[p, pl.ds(lands[p], piece), :]
            copy = pltpu.make_async_remote_copy(
                src_ref=acc_ref.at[pl.ds(pl.multiple_of(base[p] + index * piece, 8), piece), :],
                dst_ref=land,
                send_sem=rs_send.at[p, slot],
                recv_sem=rs_recv.at[p, slot],
                device_id=device,
                device_id_type=MESH,
            )
            copy.start()
            copies.append((copy, lands[p]))
            lands[p] += piece
        return copies, piece, axis

    def scatter_finish(p, started):
        copies, piece, axis = started
        marks[p].append((base[p], length[p], axis))
        base[p] = pl.multiple_of(base[p] + at[axis] * piece, 8)
        length[p] = piece
        rows = pl.ds(base[p], piece)
        value = acc_ref[rows, :]
        for copy, where in copies:
            copy.wait_recv()
            value = value + land_ref[p, where : where + piece, :]
        if len(marks[p]) < 4:
            acc_ref[rows, :] = value
        else:
            out_ref[rows, :] = value
        sent.extend(copy for copy, where in copies)

    def gather_start(p):
        whole_base, whole_length, axis = marks[p][-1]
        rows = pl.ds(base[p], length[p])
        copies = []
        for d in range(1, size[axis]):
            index, device = peer(axis, d)
            slot = slots[p]
            slots[p] += 1
            copy = pltpu.make_async_remote_copy(
                src_ref=out_ref.at[rows, :],
                dst_ref=out_ref.at[rows, :],
                send_sem=ag_send.at[p, slot],
                recv_sem=ag_recv.at[p, slot],
                device_id=device,
                device_id_type=MESH,
            )
            copy.start()
            copies.append(copy)
        return copies

    def gather_finish(p, copies):
        for copy in copies:
            copy.wait_recv()
        sent.extend(copies)
        base[p], length[p], axis = marks[p].pop()

    sent = []
    lands = [0] * PIECES
    flying = [scatter_start(p, 0) for p in range(PIECES)]
    for stage in range(4):
        for p in range(PIECES):
            scatter_finish(p, flying[p])
            if stage < 3:
                flying[p] = scatter_start(p, stage + 1)
            else:
                slots[p] = 0
                flying[p] = gather_start(p)
    for stage in range(4):
        for p in range(PIECES):
            gather_finish(p, flying[p])
            if stage < 3:
                flying[p] = gather_start(p)
    for copy in sent:
        copy.wait_send()


def summed(strips, sizes):
    size_z, size_x, size_y = sizes
    unit = 2 * PIECES * 8 * size_z * size_x * size_y
    total = -(-len(TILES) * NB // unit) * unit
    sends = size_z + size_x + size_y - 2
    length = total // PIECES
    landing = 0
    for n in (2, size_x, size_y, size_z):
        landing += length // n * (n - 1)
        length //= n
    return pl.pallas_call(
        functools.partial(sum_kernel, sizes),
        out_shape=jax.ShapeDtypeStruct((total, NB), jnp.float32),
        in_specs=[pl.BlockSpec(memory_space=pltpu.VMEM)] * len(strips),
        out_specs=pl.BlockSpec(memory_space=pltpu.VMEM),
        scratch_shapes=[
            pltpu.VMEM((total, NB), jnp.float32),
            pltpu.VMEM((PIECES, landing, NB), jnp.float32),
            pltpu.SemaphoreType.DMA((PIECES, sends)),
            pltpu.SemaphoreType.DMA((PIECES, sends)),
            pltpu.SemaphoreType.DMA((PIECES, sends)),
            pltpu.SemaphoreType.DMA((PIECES, sends)),
        ],
        compiler_params=pltpu.CompilerParams(
            collective_id=0, has_side_effects=True, vmem_limit_bytes=48 * 1024 * 1024
        ),
        cost_estimate=pl.CostEstimate(flops=total * NB, bytes_accessed=16 * total * NB, transcendentals=0),
    )(*strips)


def factor_tile(state):
    lane = lax.broadcasted_iota(jnp.int32, (8, NB), 1)
    sub = lax.broadcasted_iota(jnp.int32, (8, NB), 0)
    upper, inverse = [], []
    for s in range(NB // 8):
        base = 8 * s
        rows = state[s]
        here = (lane >= base) & (lane < base + 8)
        cols = [jnp.broadcast_to(rows[:, base + k : base + k + 1], (8, NB)) for k in range(8)]
        fwd = rows
        merged = jnp.where(here, (lane - base == sub).astype(jnp.float32), rows)
        fwd_inv = merged
        jordan = merged
        pivots = cols[0]
        pivot = jnp.broadcast_to(cols[0][0:1, :], (8, NB))
        for j in range(8):
            pivots = jnp.where(sub == j, pivot, pivots)
            reciprocal = 1.0 / pivot
            masked = jnp.where(sub == j, 0.0, cols[j])
            scaled = cols[j] * reciprocal
            both = masked * reciprocal
            if j < 7:
                corner = jnp.broadcast_to(cols[j + 1][j + 1 : j + 2, :], (8, NB))
                across = jnp.broadcast_to(cols[j + 1][j : j + 1, :], (8, NB))
                down = jnp.broadcast_to(cols[j][j + 1 : j + 2, :], (8, NB))
                pivot = corner - (down * across) * reciprocal
            for k in range(j + 1, 8):
                cols[k] = cols[k] - both * jnp.broadcast_to(cols[k][j : j + 1, :], (8, NB))
            below = jnp.where(sub > j, scaled, 0.0)
            fwd = fwd - below * jnp.broadcast_to(fwd[j : j + 1, :], (8, NB))
            fwd_inv = fwd_inv - below * jnp.broadcast_to(fwd_inv[j : j + 1, :], (8, NB))
            jordan = jordan - both * jnp.broadcast_to(jordan[j : j + 1, :], (8, NB))
        root = lax.rsqrt(pivots)
        root = root * (1.5 - 0.5 * pivots * root * root)
        upper.append(jnp.where(lane >= sub + base, fwd * root, 0.0))
        inverse.append(jnp.where(lane <= sub + base, fwd_inv * root, 0.0))
        solved = jordan * (root * root)
        solved_rows = [jnp.broadcast_to(solved[k : k + 1, :], (8, NB)) for k in range(8)]
        for r in range(s + 1, NB // 8):
            old = state[r]
            new = jnp.where(here, 0.0, old)
            for k in range(8):
                new = new - jnp.broadcast_to(old[:, base + k : base + k + 1], (8, NB)) * solved_rows[k]
            state[r] = new
    return upper, inverse


def cholesky_kernel(scale, *refs):
    packed_ref, a_ref, inv_ref, left_ref, right_ref = refs
    a_ref[...] = jnp.zeros_like(a_ref)
    for t, (i, j) in enumerate(TILES):
        a_ref[i * NB : (i + 1) * NB, j * NB : (j + 1) * NB] = packed_ref[t * NB : (t + 1) * NB, :] * scale

    def panel(k, carry):
        top = pl.multiple_of(k * NB, NB)
        rows = pl.ds(top, NB)
        state = [a_ref[pl.ds(top + 8 * s, 8), pl.ds(top, NB)] for s in range(NB // 8)]
        upper, inverse = factor_tile(state)
        for s in range(NB // 8):
            inv_ref[8 * s : 8 * s + 8, :] = inverse[s]
        def solve(i, carry):
            at = pl.multiple_of(i * TB, TB)
            part = pl.ds(at, TB)
            solved = jnp.dot(
                inv_ref[...], a_ref[rows, part], precision=lax.Precision.HIGHEST, preferred_element_type=jnp.float32
            )
            col = lax.broadcasted_iota(jnp.int32, (NB, TB), 1) + at
            solved = jnp.where(col >= top + NB, solved, 0.0)
            a_ref[rows, part] = solved
            high = solved.astype(jnp.bfloat16)
            low = (solved - high.astype(jnp.float32)).astype(jnp.bfloat16)
            right_ref[0:NB, part] = high
            right_ref[NB : 2 * NB, part] = low
            right_ref[2 * NB : 3 * NB, part] = high
            right_ref[3 * NB : 4 * NB, part] = low
            turned = solved.T
            high = turned.astype(jnp.bfloat16)
            low = (turned - high.astype(jnp.float32)).astype(jnp.bfloat16)
            left_ref[part, 0:NB] = high
            left_ref[part, NB : 2 * NB] = high
            left_ref[part, 2 * NB : 3 * NB] = low
            left_ref[part, 3 * NB : 4 * NB] = low
            return carry

        lax.fori_loop(k // (TB // NB), N // TB, solve, 0)
        for s in range(NB // 8):
            a_ref[pl.ds(top + 8 * s, 8), pl.ds(top, NB)] = upper[s]

        def update_row(i, carry):
            at = pl.multiple_of(i * TB, TB)

            def update(j, carry):
                to = pl.multiple_of(j * TB, TB)
                block = (pl.ds(at, TB), pl.ds(to, TB))
                a_ref[block] -= jnp.dot(
                    left_ref[pl.ds(at, TB), :], right_ref[:, pl.ds(to, TB)], preferred_element_type=jnp.float32
                )
                return carry

            return lax.fori_loop(i, N // TB, update, carry)

        return lax.fori_loop((k + 1) // (TB // NB), N // TB, update_row, carry)

    lax.fori_loop(0, N // NB, panel, 0)


def factor_of(packed, scale):
    return pl.pallas_call(
        functools.partial(cholesky_kernel, scale),
        out_shape=jax.ShapeDtypeStruct((N, N), jnp.float32),
        in_specs=[pl.BlockSpec(memory_space=pltpu.VMEM)],
        out_specs=pl.BlockSpec(memory_space=pltpu.VMEM),
        scratch_shapes=[
            pltpu.VMEM((NB, NB), jnp.float32),
            pltpu.VMEM((N, 4 * NB), jnp.bfloat16),
            pltpu.VMEM((4 * NB, N), jnp.bfloat16),
        ],
        compiler_params=pltpu.CompilerParams(vmem_limit_bytes=48 * 1024 * 1024),
        cost_estimate=pl.CostEstimate(flops=8 * N * N * N // 3, bytes_accessed=8 * N * N, transcendentals=0),
    )(packed)


def gram_strips(rotated):
    return [
        lax.dot_general(
            rotated[:, at : at + TB],
            rotated[:, at:],
            (((0,), (0,)), ((), ())),
            preferred_element_type=jnp.float32,
        )
        for at in range(0, N, TB)
    ]


PARTS = 2


def shards(records, offsets, column_map, angles):
    total_rows = records.shape[0] * lax.axis_size("tm")
    rows = records.shape[0] // PARTS
    blocks = offsets.shape[0] // PARTS
    strips = None
    for part in range(PARTS):
        filtered = drift_filter(
            records[part * rows : (part + 1) * rows], offsets[part * blocks : (part + 1) * blocks]
        )
        regrouped = lax.all_to_all(filtered, "gauge", split_axis=0, concat_axis=1, tiled=True)
        rotated = rosette_rotate(regrouped, column_map, angles)
        terms = gram_strips(rotated)
        strips = terms if strips is None else [one + other for one, other in zip(strips, terms)]
    size_y = lax.axis_size("gauge") // 2
    sizes = (lax.axis_size("tm") // size_y, size_y, size_y)
    return factor_of(summed(strips, sizes), 1.0 / total_rows)


def solution(mesh):
    placed = (P("tm", "gauge"), P("tm"), P(), P())
    return jax.shard_map(shards, mesh=mesh, in_specs=placed, out_specs=P(), check_vma=False)
```
